32 devices in a mesh: parts: 2 (over y), dp: 4 (over x, core), tensor: 4 (over z).
Axes of the slice: x: 2, y: 2, z: 4, core: 2. Of those that a mesh axis runs over, the one named last changes fastest.
Arguments:
- tokens: bfloat16 [16384, 8192], P(('parts', 'dp'), 'tensor'), parts along dimension 0, may hold values from -6 to 6
- target: bfloat16 [16384, 1024], P(('parts', 'dp'), 'tensor'), parts along dimension 0, may hold values from -6 to 6
- task_embed: bfloat16 [64, 2048], P('parts'), parts along dimension 0, may hold values from -6 to 6
- head_a: bfloat16 [2048, 16, 8192], P(None, 'dp', 'tensor'), may hold values from -0.0014648438 to 0.0014648438
- head_b: bfloat16 [2048, 16, 1024], P(None, 'dp', 'tensor'), may hold values from -0.00390625 to 0.00390625
- base_v: bfloat16 [8192, 1024], P('tensor', 'dp'), may hold values from -0.0625 to 0.0625
- block_tenant: int32 [128], P('parts'), parts along dimension 0, may hold values from 0 to 31, as said below
- block_count: int32 [64], P('parts'), parts along dimension 0, may hold values from 1 to 16, as said below
Outputs:
- grad_head_a: bfloat16 [4096, 16, 8192], P('parts', 'dp', 'tensor'), parts along dimension 0
- grad_head_b: bfloat16 [4096, 16, 1024], P('parts', 'dp', 'tensor'), parts along dimension 0
The draws below stay inside these ranges and needn't reach their ends.
There are 2 independent parts, one for each index of `parts`. The reference program is written for one: setup_inputs(seed, part) draws one part's arguments, and reference() takes and returns one part's arrays. A program takes and returns all parts, laid end to end along the dimension named above; an argument that names none is the same for every part. Nothing has to cross between parts.
Inputs may be any that keep to these rules, and one draw needn't show every extreme that they name: `block_tenant`: entries i * 16 to (i + 1) * 16 - 1 are the blocks of group i of dp. All blocks of a tenant lie in one group, and every tenant has a block. A group holds 1 to 15 tenants; some group holds exactly 15 and some exactly 1; groups 2i and 2i + 1 hold 16 tenants together. block_count[t] is the number of entries of block_tenant equal to t.
All inputs are finite; a program needn't handle non-finite values.
Results may differ from the reference program's by a relative error of at most 0.018.
Values may be sent and summed in bfloat16 or wider, within the bound.
A program may use at most 256 MiB of HBM per device.

```python
import jax
import jax.numpy as jnp
from jax import lax

D = 8192
KV = 1024
H = 2048
R = 16
BLOCK = 128
TEN_GRP = 8
BLK = 16
T_SIZE = 32
ROWS = 8192
N_DP = 4


def tenant_layout(key):
    pair_count = N_DP // 2
    keys = jax.random.split(key, 6)
    shift = jax.random.randint(keys[0], (pair_count,), 0, TEN_GRP)
    forced = jax.random.randint(keys[1], (), 0, pair_count)
    shift = jnp.where(jnp.arange(pair_count) == forced, TEN_GRP - 1, shift)
    flip = 1 - 2 * jax.random.randint(keys[2], (pair_count,), 0, 2)
    sizes = jnp.stack([TEN_GRP + flip * shift, TEN_GRP - flip * shift], axis=1).reshape(N_DP)
    ends = jnp.cumsum(sizes)
    starts = ends - sizes
    position = jnp.arange(T_SIZE)
    group_of_position = jnp.sum((position[:, None] >= ends[None, :]).astype(jnp.int32), axis=1)
    shuffle = jax.random.permutation(keys[3], T_SIZE)
    owner = jnp.zeros((T_SIZE,), jnp.int32).at[shuffle].set(group_of_position.astype(jnp.int32))
    ordered = jnp.argsort(owner * T_SIZE + jnp.arange(T_SIZE), stable=True)
    column = jnp.arange(BLK)
    extra = jax.random.randint(keys[4], (N_DP, BLK), 0, 1048576) % sizes[:, None]
    local = jnp.where(column[None, :] < sizes[:, None], column[None, :], extra)
    chosen = ordered[starts[:, None] + local]
    order_keys = jax.random.split(keys[5], N_DP)
    chosen = jax.vmap(jax.random.permutation)(order_keys, chosen)
    return chosen.reshape(N_DP * BLK).astype(jnp.int32)


def draw_block_tenant(key, part):
    return tenant_layout(key)


def draw_block_count(key, part):
    chosen = tenant_layout(key)
    match = chosen[None, :] == jnp.arange(T_SIZE)[:, None]
    return jnp.sum(match.astype(jnp.int32), axis=1).astype(jnp.int32)


def levels(own_key, shape, cuts, smallest, high):
    gain, own = 1.0, jax.random.fold_in(own_key, 6)
    for axis_at, shards_of in cuts:
        heights = jnp.exp(jax.random.uniform(jax.random.fold_in(own, axis_at), (shards_of,), jnp.float32, smallest / len(cuts), high / len(cuts)))
        gain = gain * jnp.repeat(heights, shape[axis_at] // shards_of).reshape([-1 if axis == axis_at else 1 for axis in range(len(shape))])
    return gain


def centred(rng, dims, scale, bound, pieces=(), kind=jnp.bfloat16):
    values = jax.random.normal(rng, dims, jnp.float32) * scale
    if len(pieces) > 0:
        values = levels(rng, dims, pieces, -0.22, 0.18) * values
    return jnp.clip(values, min=-bound, max=bound).astype(kind)


def setup_inputs(seed: int = 0, part: int = 0) -> dict:
    key_list = jax.random.split(jax.random.key(seed), 9)
    part_keys = jax.random.split(jax.random.fold_in(key_list[8], part), 9)
    tokens = centred(part_keys[0], (ROWS, D), 1.0, 6.0, ((0, 4), (1, 4)))
    target = centred(part_keys[1], (ROWS, KV), 1.0, 6.0, ((0, 4), (1, 4)))
    task_embed = centred(part_keys[2], (T_SIZE, H), 1.0, 6.0)
    head_a = centred(key_list[3], (H, R, D), (H * D) ** -0.5, 0.0014648438, ((1, 4), (2, 4)))
    head_b = centred(key_list[4], (H, R, KV), (H * KV) ** -0.5, 0.00390625, ((1, 4), (2, 4)))
    base_v = centred(key_list[5], (D, KV), D ** -0.5, 0.0625, ((0, 4), (1, 4)))
    block_tenant = draw_block_tenant(jax.random.fold_in(jax.random.fold_in(key_list[8], part), 71), part)
    block_count = draw_block_count(jax.random.fold_in(jax.random.fold_in(key_list[8], part), 71), part)
    return dict(tokens=tokens, target=target, task_embed=task_embed, head_a=head_a, head_b=head_b, base_v=base_v, block_tenant=block_tenant, block_count=block_count)


def reference(tokens, target, task_embed, head_a, head_b, base_v, block_tenant, block_count):
    tenants = task_embed.shape[0]
    flat_a = jnp.dot(task_embed, head_a.reshape(H, R * D), preferred_element_type=jnp.float32)
    flat_a = flat_a.astype(jnp.bfloat16).reshape(tenants, R, D)
    flat_b = jnp.dot(task_embed, head_b.reshape(H, R * KV), preferred_element_type=jnp.float32)
    flat_b = flat_b.astype(jnp.bfloat16).reshape(tenants, R, KV)
    blocks_all = block_tenant.shape[0]
    x_blocks = tokens.reshape(blocks_all, BLOCK, D)
    factor_a = flat_a[block_tenant]
    factor_b = flat_b[block_tenant]
    low_rank = jnp.einsum("brd,bmd->brm", factor_a.astype(jnp.float32), x_blocks.astype(jnp.float32))
    low_rank = low_rank.astype(jnp.bfloat16)
    base = jnp.dot(tokens, base_v, preferred_element_type=jnp.float32).reshape(blocks_all, BLOCK, KV)
    adapted = jnp.einsum("brm,brc->bmc", low_rank.astype(jnp.float32), factor_b.astype(jnp.float32))
    projected = base + 2.0 * adapted
    weight = 1.0 / (BLOCK * block_count[block_tenant].astype(jnp.float32))
    error = projected - target.reshape(blocks_all, BLOCK, KV).astype(jnp.float32)
    error_grad = (error * weight[:, None, None]).astype(jnp.bfloat16)
    rank_grad = jnp.einsum("bmc,brc->brm", error_grad.astype(jnp.float32), factor_b.astype(jnp.float32))
    rank_grad = rank_grad.astype(jnp.bfloat16)
    block_grad_a = 2.0 * jnp.einsum("brm,bmd->brd", rank_grad.astype(jnp.float32), x_blocks.astype(jnp.float32))
    block_grad_b = 2.0 * jnp.einsum("brm,bmc->brc", low_rank.astype(jnp.float32), error_grad.astype(jnp.float32))
    member = (block_tenant[None, :] == jnp.arange(tenants, dtype=jnp.int32)[:, None]).astype(jnp.float32)
    grad_a = jnp.dot(member, block_grad_a.reshape(blocks_all, R * D), precision=lax.Precision.HIGHEST)
    grad_b = jnp.dot(member, block_grad_b.reshape(blocks_all, R * KV), precision=lax.Precision.HIGHEST)
    grad_a = grad_a.astype(jnp.bfloat16)
    grad_b = grad_b.astype(jnp.bfloat16)
    grad_head_a = jnp.dot(task_embed.T, grad_a, preferred_element_type=jnp.float32)
    grad_head_b = jnp.dot(task_embed.T, grad_b, preferred_element_type=jnp.float32)
    grad_head_a = grad_head_a.astype(jnp.bfloat16).reshape(H, R, D)
    grad_head_b = grad_head_b.astype(jnp.bfloat16).reshape(H, R, KV)
    return (grad_head_a, grad_head_b)
```

```python
import functools

import jax
import jax.numpy as jnp
from jax import lax
from jax.experimental import pallas as pl
from jax.experimental.pallas import tpu as pltpu
from jax.sharding import PartitionSpec as P

R = 16
BLOCK = 128
SLOTS = 16
STEP = 256
F32 = jnp.float32
BF16 = jnp.bfloat16


def owner_tables(block_tenant, tenants, blocks, groups):
    ids = jnp.arange(tenants, dtype=jnp.int32)
    block_group = jnp.arange(blocks * groups, dtype=jnp.int32) // blocks
    member = block_tenant[None, :] == ids[:, None]
    owner = jnp.max(jnp.where(member, block_group[None, :], -1), axis=1)
    earlier = (owner[None, :] == owner[:, None]) & (ids[None, :] < ids[:, None])
    slot = jnp.sum(earlier.astype(jnp.int32), axis=1)
    group_ids = jnp.arange(groups, dtype=jnp.int32)
    slot_ids = jnp.arange(SLOTS, dtype=jnp.int32)
    place = (owner[None, None, :] == group_ids[:, None, None]) & (
        slot[None, None, :] == slot_ids[None, :, None]
    )
    return place


def dot(a, b):
    return jnp.dot(a, b, preferred_element_type=F32)


def dot_nt(a, b):
    return lax.dot_general(a, b, (((1,), (1,)), ((), ())), preferred_element_type=F32)


def generate_kernel(count, embed_ref, head_ref, out_ref, total):
    step = pl.program_id(0)
    part, ranks, width = head_ref.shape
    rows = embed_ref.shape[0]

    @pl.when(step == 0)
    def _():
        total[...] = jnp.zeros_like(total)

    spread = lax.broadcasted_iota(jnp.int32, (part, part * ranks), 0) == (
        lax.broadcasted_iota(jnp.int32, (part, part * ranks), 1) // ranks
    )
    wide = dot(embed_ref[...], spread.astype(F32).astype(BF16))
    row = lax.broadcasted_iota(jnp.int32, wide.shape, 0)
    col = lax.broadcasted_iota(jnp.int32, wide.shape, 1)
    wide = jnp.where((row // count) % ranks == col % ranks, wide, 0.0).astype(BF16)
    total[...] += dot(wide, head_ref[...].reshape(part * ranks, width))

    @pl.when(step == pl.num_programs(0) - 1)
    def _():
        out_ref[...] = total[...].astype(BF16)


def generate(embed, head, count):
    hidden, ranks, width = head.shape
    rows = embed.shape[0]
    return pl.pallas_call(
        functools.partial(generate_kernel, count),
        grid=(hidden // STEP,),
        in_specs=[
            pl.BlockSpec((rows, STEP), lambda i: (0, i)),
            pl.BlockSpec((STEP, ranks, width), lambda i: (i, 0, 0)),
        ],
        out_specs=pl.BlockSpec((rows, width), lambda i: (0, 0)),
        out_shape=jax.ShapeDtypeStruct((rows, width), BF16),
        scratch_shapes=[pltpu.VMEM((rows, width), F32)],
        compiler_params=pltpu.CompilerParams(vmem_limit_bytes=40 * 2**20),
        cost_estimate=pl.CostEstimate(
            flops=2 * rows * hidden * ranks * width,
            bytes_accessed=2 * hidden * ranks * width,
            transcendentals=0,
        ),
    )(embed, head)


def head_grad_kernel(embed_ref, grad_ref, out_ref):
    part, ranks, width = out_ref.shape
    spread = (
        lax.broadcasted_iota(jnp.int32, (part * ranks, part), 0) // ranks
    ) == lax.broadcasted_iota(jnp.int32, (part * ranks, part), 1)
    wide = dot(spread.astype(F32).astype(BF16), embed_ref[...])
    row = lax.broadcasted_iota(jnp.int32, wide.shape, 0)
    col = lax.broadcasted_iota(jnp.int32, wide.shape, 1)
    wide = jnp.where((col // SLOTS) % ranks == row % ranks, wide, 0.0).astype(BF16)
    out = dot(wide, grad_ref[...]).astype(BF16)
    out_ref[...] = out.reshape(part, ranks, width)


def head_grad(embed, grad, ranks):
    hidden, depth = embed.shape
    width = grad.shape[1]
    return pl.pallas_call(
        head_grad_kernel,
        grid=(hidden // STEP,),
        in_specs=[
            pl.BlockSpec((STEP, depth), lambda i: (i, 0)),
            pl.BlockSpec((depth, width), lambda i: (0, 0)),
        ],
        out_specs=pl.BlockSpec((STEP, ranks, width), lambda i: (i, 0, 0)),
        out_shape=jax.ShapeDtypeStruct((hidden, ranks, width), BF16),
        compiler_params=pltpu.CompilerParams(vmem_limit_bytes=40 * 2**20),
        cost_estimate=pl.CostEstimate(
            flops=2 * hidden * ranks * depth * width,
            bytes_accessed=2 * hidden * ranks * width,
            transcendentals=0,
        ),
    )(embed, grad)


def body(tokens, target, task_embed, head_a, head_b, base_v, block_tenant, block_count):
    groups = lax.axis_size("dp")
    group_now = lax.axis_index("dp")
    tenants, hidden = task_embed.shape
    rank_part = head_a.shape[1]
    width = head_a.shape[2]
    kv_part = head_b.shape[2]
    rows = tokens.shape[0]
    blocks = rows // BLOCK

    every_v = lax.all_gather(base_v, "dp", axis=0)

    embed_rows = jnp.tile(task_embed, (rank_part, 1))
    flat_b = generate(embed_rows, head_b, tenants)
    every_b = lax.all_gather(flat_b, ("dp", "tensor"), axis=0)

    place = owner_tables(block_tenant, tenants, blocks, groups)
    place_bf = place.astype(BF16)
    slot_rows = dot(place_bf.reshape(groups * SLOTS, tenants), task_embed).astype(BF16)
    slot_rows = jnp.broadcast_to(
        slot_rows.reshape(groups, 1, SLOTS, hidden), (groups, rank_part, SLOTS, hidden)
    ).reshape(groups * rank_part * SLOTS, hidden)
    slot_cols = slot_rows.T

    flat_a = generate(slot_rows, head_a, SLOTS)
    own_a = lax.all_to_all(
        flat_a.reshape(groups, rank_part * SLOTS, width), "dp", 0, 0, tiled=True
    ).reshape(R * SLOTS, width)

    mine = lax.dynamic_index_in_dim(place_bf, group_now, 0, keepdims=False)
    shards = every_b.shape[0] // groups
    every_b = every_b.reshape(groups, shards, rank_part, tenants, kv_part)
    own_b = jnp.einsum("st,dxrtc->drsxc", mine, every_b, preferred_element_type=F32)
    own_b = own_b.astype(BF16).reshape(R, SLOTS, shards * kv_part)
    kv = shards * kv_part
    own_b_cols = lax.dynamic_slice_in_dim(own_b, lax.axis_index("tensor") * kv_part, kv_part, 2)
    own_b_cols = own_b_cols.reshape(R * SLOTS, kv_part)
    flat_own_b = own_b.reshape(R * SLOTS, kv)
    full_v = jnp.transpose(every_v, (1, 0, 2)).reshape(width, kv)
    gram_b = jnp.einsum("rsc,qsc->srq", own_b, own_b, preferred_element_type=F32)
    through = dot_nt(flat_own_b, full_v).astype(BF16)

    own_blocks = lax.dynamic_slice_in_dim(block_tenant, group_now * blocks, blocks)
    tenant_hot = own_blocks[:, None] == jnp.arange(tenants, dtype=jnp.int32)[None, :]
    pick = jnp.sum(
        (mine.astype(F32)[:, None, :] * tenant_hot[None, :, :].astype(F32)), axis=2
    )
    count = block_count.astype(F32)
    slot_count = jnp.sum(mine.astype(F32) * count[None, :], axis=1)
    slot_weight = 1.0 / (BLOCK * jnp.maximum(slot_count, 1.0))
    block_weight = 1.0 / (BLOCK * jnp.sum(jnp.where(tenant_hot, count[None, :], 0.0), axis=1))

    pick_rows = jnp.repeat(pick, BLOCK, axis=1)
    partial_l = dot_nt(own_a, tokens).reshape(R, SLOTS, rows)
    partial_z = (dot_nt(through, tokens) - dot_nt(own_b_cols, target)).reshape(R, SLOTS, rows)
    partial_l = jnp.sum(partial_l * pick_rows[None], axis=1)
    partial_z = jnp.sum(partial_z * pick_rows[None], axis=1)
    both = jnp.concatenate([partial_l, partial_z], axis=0).astype(BF16)
    both = lax.psum(both, "tensor")
    low_rank = both[:R]
    back = both[R:].astype(F32).reshape(R, blocks, BLOCK)
    low_blocks = low_rank.reshape(R, blocks, BLOCK)
    gram_block = jnp.einsum(
        "sb,srq->brq", pick, gram_b, precision=lax.Precision.HIGHEST
    )
    cross = jnp.einsum(
        "brq,qbm->rbm", gram_block.astype(BF16), low_blocks, preferred_element_type=F32
    )
    rank_grad = (back + 2.0 * cross) * block_weight[None, :, None]
    rank_grad = rank_grad.astype(BF16).reshape(R, rows)

    pick_bf = pick_rows.astype(BF16)
    spread_g = (rank_grad[:, None, :] * pick_bf[None]).reshape(R * SLOTS, rows)
    spread_l = (low_rank[:, None, :] * pick_bf[None]).reshape(R * SLOTS, rows)
    grad_a = (2.0 * dot(spread_g, tokens)).astype(BF16)
    every_a = lax.all_to_all(
        grad_a.reshape(groups, rank_part * SLOTS, width), "dp", 0, 0, tiled=True
    ).reshape(groups * rank_part * SLOTS, width)

    low_x = dot(spread_l, tokens).astype(BF16)
    grad_b = dot(low_x, full_v).astype(BF16)
    grad_b = lax.psum_scatter(grad_b, "tensor", scatter_dimension=1, tiled=True).astype(F32)
    gram_l = jnp.einsum("rbm,qbm->brq", low_blocks, low_blocks, preferred_element_type=F32)
    gram_l = jnp.einsum("sb,brq->srq", pick, gram_l, precision=lax.Precision.HIGHEST)
    adapted = jnp.einsum(
        "srq,qsc->rsc",
        gram_l.astype(BF16),
        own_b_cols.reshape(R, SLOTS, kv_part),
        preferred_element_type=F32,
    )
    grad_b = grad_b - dot(spread_l, target)
    grad_b = grad_b.reshape(R, SLOTS, kv_part) + 2.0 * adapted
    grad_b = (2.0 * grad_b * slot_weight[None, :, None]).astype(BF16)
    every_gb = lax.all_to_all(
        grad_b.reshape(groups, rank_part * SLOTS, kv_part), "dp", 0, 0, tiled=True
    ).reshape(groups * rank_part * SLOTS, kv_part)

    grad_head_b = head_grad(slot_cols, every_gb, rank_part)
    grad_head_a = head_grad(slot_cols, every_a, rank_part)
    return (grad_head_a, grad_head_b)


def solution(mesh):
    return jax.shard_map(
        body,
        mesh=mesh,
        in_specs=(
            P(("parts", "dp"), "tensor"),
            P(("parts", "dp"), "tensor"),
            P("parts", None),
            P(None, "dp", "tensor"),
            P(None, "dp", "tensor"),
            P("tensor", "dp"),
            P("parts"),
            P("parts"),
        ),
        out_specs=(P("parts", "dp", "tensor"), P("parts", "dp", "tensor")),
        check_vma=False,
    )
```

```python
import functools

import jax
import jax.numpy as jnp
from jax import lax
from jax.experimental import pallas as pl
from jax.experimental.pallas import tpu as pltpu
from jax.sharding import PartitionSpec as P

R = 16
BLOCK = 128
SLOTS = 16
STEP = 256
F32 = jnp.float32
BF16 = jnp.bfloat16


def owner_tables(block_tenant, tenants, blocks, groups):
    ids = jnp.arange(tenants, dtype=jnp.int32)
    block_group = jnp.arange(blocks * groups, dtype=jnp.int32) // blocks
    member = block_tenant[None, :] == ids[:, None]
    owner = jnp.max(jnp.where(member, block_group[None, :], -1), axis=1)
    earlier = (owner[None, :] == owner[:, None]) & (ids[None, :] < ids[:, None])
    slot = jnp.sum(earlier.astype(jnp.int32), axis=1)
    group_ids = jnp.arange(groups, dtype=jnp.int32)
    slot_ids = jnp.arange(SLOTS, dtype=jnp.int32)
    place = (owner[None, None, :] == group_ids[:, None, None]) & (
        slot[None, None, :] == slot_ids[None, :, None]
    )
    return place


def dot(a, b):
    return jnp.dot(a, b, preferred_element_type=F32)


def dot_nt(a, b):
    return lax.dot_general(a, b, (((1,), (1,)), ((), ())), preferred_element_type=F32)


def generate_kernel(count, embed_ref, head_ref, out_ref, total):
    step = pl.program_id(0)
    part, ranks, width = head_ref.shape
    rows = embed_ref.shape[0]

    @pl.when(step == 0)
    def _():
        total[...] = jnp.zeros_like(total)

    spread = lax.broadcasted_iota(jnp.int32, (part, part * ranks), 0) == (
        lax.broadcasted_iota(jnp.int32, (part, part * ranks), 1) // ranks
    )
    wide = dot(embed_ref[...], spread.astype(F32).astype(BF16))
    row = lax.broadcasted_iota(jnp.int32, wide.shape, 0)
    col = lax.broadcasted_iota(jnp.int32, wide.shape, 1)
    wide = jnp.where((row // count) % ranks == col % ranks, wide, 0.0).astype(BF16)
    total[...] += dot(wide, head_ref[...].reshape(part * ranks, width))

    @pl.when(step == pl.num_programs(0) - 1)
    def _():
        out_ref[...] = total[...].astype(BF16)


def generate(embed, head, count):
    hidden, ranks, width = head.shape
    rows = embed.shape[0]
    return pl.pallas_call(
        functools.partial(generate_kernel, count),
        grid=(hidden // STEP,),
        in_specs=[
            pl.BlockSpec((rows, STEP), lambda i: (0, i)),
            pl.BlockSpec((STEP, ranks, width), lambda i: (i, 0, 0)),
        ],
        out_specs=pl.BlockSpec((rows, width), lambda i: (0, 0)),
        out_shape=jax.ShapeDtypeStruct((rows, width), BF16),
        scratch_shapes=[pltpu.VMEM((rows, width), F32)],
        compiler_params=pltpu.CompilerParams(vmem_limit_bytes=40 * 2**20),
        cost_estimate=pl.CostEstimate(
            flops=2 * rows * hidden * ranks * width,
            bytes_accessed=2 * hidden * ranks * width,
            transcendentals=0,
        ),
    )(embed, head)


def spread_kernel(ranks, embed_ref, out_ref):
    part, depth = embed_ref.shape
    spread = (
        lax.broadcasted_iota(jnp.int32, (part * ranks, part), 0) // ranks
    ) == lax.broadcasted_iota(jnp.int32, (part * ranks, part), 1)
    wide = dot(spread.astype(F32).astype(BF16), embed_ref[...])
    row = lax.broadcasted_iota(jnp.int32, wide.shape, 0)
    col = lax.broadcasted_iota(jnp.int32, wide.shape, 1)
    out_ref[...] = jnp.where((col // SLOTS) % ranks == row % ranks, wide, 0.0).astype(BF16)


def spread_embed(embed, ranks):
    hidden, depth = embed.shape
    return pl.pallas_call(
        functools.partial(spread_kernel, ranks),
        grid=(hidden // STEP,),
        in_specs=[pl.BlockSpec((STEP, depth), lambda i: (i, 0))],
        out_specs=pl.BlockSpec((STEP * ranks, depth), lambda i: (i, 0)),
        out_shape=jax.ShapeDtypeStruct((hidden * ranks, depth), BF16),
        compiler_params=pltpu.CompilerParams(vmem_limit_bytes=24 * 2**20),
        cost_estimate=pl.CostEstimate(
            flops=2 * hidden * ranks * depth * STEP,
            bytes_accessed=2 * hidden * ranks * depth,
            transcendentals=0,
        ),
    )(embed)


def head_grad_kernel(wide_ref, grad_ref, out_ref):
    part, ranks, width = out_ref.shape
    out = dot(wide_ref[...], grad_ref[...]).astype(BF16)
    out_ref[...] = out.reshape(part, ranks, width)


def head_grad(wide, grad, ranks):
    depth = wide.shape[1]
    hidden = wide.shape[0] // ranks
    width = grad.shape[1]
    return pl.pallas_call(
        head_grad_kernel,
        grid=(hidden // STEP,),
        in_specs=[
            pl.BlockSpec((STEP * ranks, depth), lambda i: (i, 0)),
            pl.BlockSpec((depth, width), lambda i: (0, 0)),
        ],
        out_specs=pl.BlockSpec((STEP, ranks, width), lambda i: (i, 0, 0)),
        out_shape=jax.ShapeDtypeStruct((hidden, ranks, width), BF16),
        compiler_params=pltpu.CompilerParams(vmem_limit_bytes=40 * 2**20),
        cost_estimate=pl.CostEstimate(
            flops=2 * hidden * ranks * depth * width,
            bytes_accessed=2 * hidden * ranks * width,
            transcendentals=0,
        ),
    )(wide, grad)


def gather_all(x, axis):
    shards = lax.axis_size(axis)
    return lax.all_to_all(jnp.broadcast_to(x[None], (shards,) + x.shape), axis, 0, 0, tiled=True)


def body(tokens, target, task_embed, head_a, head_b, base_v, block_tenant, block_count):
    groups = lax.axis_size("dp")
    group_now = lax.axis_index("dp")
    tenants, hidden = task_embed.shape
    rank_part = head_a.shape[1]
    width = head_a.shape[2]
    kv_part = head_b.shape[2]
    rows = tokens.shape[0]
    blocks = rows // BLOCK

    shards = lax.axis_size("tensor")
    shard_now = lax.axis_index("tensor")
    full_v = lax.all_gather(base_v, "dp", axis=1, tiled=True)
    kv = full_v.shape[1]

    place = owner_tables(block_tenant, tenants, blocks, groups)
    place_bf = place.astype(BF16)
    slot_rows = dot(place_bf.reshape(groups * SLOTS, tenants), task_embed).astype(BF16)
    slot_rows = jnp.broadcast_to(
        slot_rows.reshape(groups, 1, SLOTS, hidden), (groups, rank_part, SLOTS, hidden)
    ).reshape(groups * rank_part * SLOTS, hidden)

    flat_b = generate(slot_rows, head_b, SLOTS)
    own_b_cols = lax.all_to_all(
        flat_b.reshape(groups, rank_part * SLOTS, kv_part), "dp", 0, 0, tiled=True
    ).reshape(R * SLOTS, kv_part)
    every_b = gather_all(own_b_cols, "tensor")
    flat_a = generate(slot_rows, head_a, SLOTS)
    own_a = lax.all_to_all(
        flat_a.reshape(groups, rank_part * SLOTS, width), "dp", 0, 0, tiled=True
    ).reshape(R * SLOTS, width)

    mine = lax.dynamic_index_in_dim(place_bf, group_now, 0, keepdims=False)
    flat_own_b = jnp.transpose(every_b, (1, 0, 2)).reshape(R * SLOTS, kv)
    own_b = flat_own_b.reshape(R, SLOTS, kv)
    gram_b = jnp.einsum("rsc,qsc->srq", own_b, own_b, preferred_element_type=F32)
    through = dot_nt(flat_own_b, full_v).astype(BF16)

    own_blocks = lax.dynamic_slice_in_dim(block_tenant, group_now * blocks, blocks)
    tenant_hot = own_blocks[:, None] == jnp.arange(tenants, dtype=jnp.int32)[None, :]
    pick = jnp.sum(
        (mine.astype(F32)[:, None, :] * tenant_hot[None, :, :].astype(F32)), axis=2
    )
    count = block_count.astype(F32)
    slot_count = jnp.sum(mine.astype(F32) * count[None, :], axis=1)
    slot_weight = 1.0 / (BLOCK * jnp.maximum(slot_count, 1.0))
    block_weight = 1.0 / (BLOCK * jnp.sum(jnp.where(tenant_hot, count[None, :], 0.0), axis=1))

    pick_rows = jnp.repeat(pick, BLOCK, axis=1)
    partial_l = dot_nt(own_a, tokens).reshape(R, SLOTS, rows)
    partial_z = (dot_nt(through, tokens) - dot_nt(own_b_cols, target)).reshape(R, SLOTS, rows)
    partial_l = jnp.sum(partial_l * pick_rows[None], axis=1)
    partial_z = jnp.sum(partial_z * pick_rows[None], axis=1)
    both = jnp.concatenate([partial_l, partial_z], axis=0).astype(BF16)
    both = jnp.sum(gather_all(both, "tensor").astype(F32), axis=0)
    low_rank = both[:R].astype(BF16)
    back = both[R:].reshape(R, blocks, BLOCK)
    low_blocks = low_rank.reshape(R, blocks, BLOCK)
    gram_block = jnp.einsum(
        "sb,srq->brq", pick, gram_b, precision=lax.Precision.HIGHEST
    )
    cross = jnp.einsum(
        "brq,qbm->rbm", gram_block.astype(BF16), low_blocks, preferred_element_type=F32
    )
    rank_grad = (back + 2.0 * cross) * block_weight[None, :, None]
    rank_grad = rank_grad.astype(BF16).reshape(R, rows)

    pick_bf = pick_rows.astype(BF16)
    spread_g = (rank_grad[:, None, :] * pick_bf[None]).reshape(R * SLOTS, rows)
    spread_l = (low_rank[:, None, :] * pick_bf[None]).reshape(R * SLOTS, rows)
    grad_a = (2.0 * dot(spread_g, tokens)).astype(BF16)
    every_a = lax.all_to_all(
        grad_a.reshape(groups, rank_part * SLOTS, width), "dp", 0, 0, tiled=True
    ).reshape(groups * rank_part * SLOTS, width)

    low_x = dot(spread_l, tokens).astype(BF16)
    gram_l = jnp.einsum("rbm,qbm->brq", low_blocks, low_blocks, preferred_element_type=F32)
    gram_l = jnp.einsum("sb,brq->srq", pick, gram_l, precision=lax.Precision.HIGHEST)
    adapted = jnp.einsum(
        "srq,qsc->rsc",
        gram_l.astype(BF16),
        own_b_cols.reshape(R, SLOTS, kv_part),
        preferred_element_type=F32,
    )
    extra = 2.0 * adapted.reshape(R * SLOTS, kv_part) - dot(spread_l, target)
    here = (jnp.arange(shards) == shard_now).astype(F32)
    scale = jnp.tile(2.0 * slot_weight, (R,))
    grad_b = dot(low_x, full_v).reshape(R * SLOTS, shards, kv_part)
    grad_b = (grad_b + here[None, :, None] * extra[:, None, :]) * scale[:, None, None]
    grad_b = grad_b.astype(BF16).reshape(groups, rank_part * SLOTS, shards, kv_part)
    grad_b = jnp.transpose(grad_b, (0, 2, 1, 3))
    grad_b = grad_b.reshape(groups * shards, rank_part * SLOTS, kv_part)
    every_gb = lax.all_to_all(grad_b, ("dp", "tensor"), 0, 0, tiled=True)
    every_gb = every_gb.reshape(groups, shards, rank_part * SLOTS, kv_part).astype(F32)
    every_gb = jnp.sum(every_gb, axis=1).astype(BF16)
    every_gb = every_gb.reshape(groups * rank_part * SLOTS, kv_part)

    wide = spread_embed(slot_rows.T, rank_part)
    grad_head_a = head_grad(wide, every_a, rank_part)
    grad_head_b = head_grad(wide, every_gb, rank_part)
    return (grad_head_a, grad_head_b)


def solution(mesh):
    return jax.shard_map(
        body,
        mesh=mesh,
        in_specs=(
            P(("parts", "dp"), "tensor"),
            P(("parts", "dp"), "tensor"),
            P("parts", None),
            P(None, "dp", "tensor"),
            P(None, "dp", "tensor"),
            P("tensor", "dp"),
            P("parts"),
            P("parts"),
        ),
        out_specs=(P("parts", "dp", "tensor"), P("parts", "dp", "tensor")),
        check_vma=False,
    )
```

```python
import functools

import jax
import jax.numpy as jnp
from jax import lax
from jax.experimental import pallas as pl
from jax.experimental.pallas import tpu as pltpu
from jax.sharding import PartitionSpec as P

R = 16
BLOCK = 128
SLOTS = 16
STEP = 256
F32 = jnp.float32
BF16 = jnp.bfloat16


def owner_tables(block_tenant, tenants, blocks, groups):
    ids = jnp.arange(tenants, dtype=jnp.int32)
    block_group = jnp.arange(blocks * groups, dtype=jnp.int32) // blocks
    member = block_tenant[None, :] == ids[:, None]
    owner = jnp.max(jnp.where(member, block_group[None, :], -1), axis=1)
    earlier = (owner[None, :] == owner[:, None]) & (ids[None, :] < ids[:, None])
    slot = jnp.sum(earlier.astype(jnp.int32), axis=1)
    group_ids = jnp.arange(groups, dtype=jnp.int32)
    slot_ids = jnp.arange(SLOTS, dtype=jnp.int32)
    place = (owner[None, None, :] == group_ids[:, None, None]) & (
        slot[None, None, :] == slot_ids[None, :, None]
    )
    return place


def dot(a, b):
    return jnp.dot(a, b, preferred_element_type=F32)


def dot_nt(a, b):
    return lax.dot_general(a, b, (((1,), (1,)), ((), ())), preferred_element_type=F32)


def generate_kernel(count, embed_ref, head_ref, out_ref, total):
    step = pl.program_id(0)
    part, ranks, width = head_ref.shape
    rows = embed_ref.shape[0]

    @pl.when(step == 0)
    def _():
        total[...] = jnp.zeros_like(total)

    spread = lax.broadcasted_iota(jnp.int32, (part, part * ranks), 0) == (
        lax.broadcasted_iota(jnp.int32, (part, part * ranks), 1) // ranks
    )
    wide = dot(embed_ref[...], spread.astype(F32).astype(BF16))
    row = lax.broadcasted_iota(jnp.int32, wide.shape, 0)
    col = lax.broadcasted_iota(jnp.int32, wide.shape, 1)
    wide = jnp.where((row // count) % ranks == col % ranks, wide, 0.0).astype(BF16)
    total[...] += dot(wide, head_ref[...].reshape(part * ranks, width))

    @pl.when(step == pl.num_programs(0) - 1)
    def _():
        out_ref[...] = total[...].astype(BF16)


def generate(embed, head, count):
    hidden, ranks, width = head.shape
    rows = embed.shape[0]
    return pl.pallas_call(
        functools.partial(generate_kernel, count),
        grid=(hidden // STEP,),
        in_specs=[
            pl.BlockSpec((rows, STEP), lambda i: (0, i)),
            pl.BlockSpec((STEP, ranks, width), lambda i: (i, 0, 0)),
        ],
        out_specs=pl.BlockSpec((rows, width), lambda i: (0, 0)),
        out_shape=jax.ShapeDtypeStruct((rows, width), BF16),
        scratch_shapes=[pltpu.VMEM((rows, width), F32)],
        compiler_params=pltpu.CompilerParams(vmem_limit_bytes=40 * 2**20),
        cost_estimate=pl.CostEstimate(
            flops=2 * rows * hidden * ranks * width,
            bytes_accessed=2 * hidden * ranks * width,
            transcendentals=0,
        ),
    )(embed, head)


def spread_kernel(ranks, embed_ref, out_ref):
    part, depth = embed_ref.shape
    spread = (
        lax.broadcasted_iota(jnp.int32, (part * ranks, part), 0) // ranks
    ) == lax.broadcasted_iota(jnp.int32, (part * ranks, part), 1)
    wide = dot(spread.astype(F32).astype(BF16), embed_ref[...])
    row = lax.broadcasted_iota(jnp.int32, wide.shape, 0)
    col = lax.broadcasted_iota(jnp.int32, wide.shape, 1)
    out_ref[...] = jnp.where((col // SLOTS) % ranks == row % ranks, wide, 0.0).astype(BF16)


def spread_embed(embed, ranks):
    hidden, depth = embed.shape
    return pl.pallas_call(
        functools.partial(spread_kernel, ranks),
        grid=(hidden // STEP,),
        in_specs=[pl.BlockSpec((STEP, depth), lambda i: (i, 0))],
        out_specs=pl.BlockSpec((STEP * ranks, depth), lambda i: (i, 0)),
        out_shape=jax.ShapeDtypeStruct((hidden * ranks, depth), BF16),
        compiler_params=pltpu.CompilerParams(vmem_limit_bytes=24 * 2**20),
        cost_estimate=pl.CostEstimate(
            flops=2 * hidden * ranks * depth * STEP,
            bytes_accessed=2 * hidden * ranks * depth,
            transcendentals=0,
        ),
    )(embed)


def head_grad_kernel(wide_ref, grad_ref, out_ref):
    part, ranks, width = out_ref.shape
    out = dot(wide_ref[...], grad_ref[...]).astype(BF16)
    out_ref[...] = out.reshape(part, ranks, width)


def head_grad(wide, grad, ranks):
    depth = wide.shape[1]
    hidden = wide.shape[0] // ranks
    width = grad.shape[1]
    return pl.pallas_call(
        head_grad_kernel,
        grid=(hidden // STEP,),
        in_specs=[
            pl.BlockSpec((STEP * ranks, depth), lambda i: (i, 0)),
            pl.BlockSpec((depth, width), lambda i: (0, 0)),
        ],
        out_specs=pl.BlockSpec((STEP, ranks, width), lambda i: (i, 0, 0)),
        out_shape=jax.ShapeDtypeStruct((hidden, ranks, width), BF16),
        compiler_params=pltpu.CompilerParams(vmem_limit_bytes=40 * 2**20),
        cost_estimate=pl.CostEstimate(
            flops=2 * hidden * ranks * depth * width,
            bytes_accessed=2 * hidden * ranks * width,
            transcendentals=0,
        ),
    )(wide, grad)


def mix_kernel(weight_ref, x_ref, out_ref):
    out_ref[...] = dot(weight_ref[...], x_ref[...]).astype(BF16)


def mix(weight, x):
    outs, rows = weight.shape
    width = x.shape[1]
    part = 256
    return pl.pallas_call(
        mix_kernel,
        grid=(width // part,),
        in_specs=[
            pl.BlockSpec((outs, rows), lambda i: (0, 0)),
            pl.BlockSpec((rows, part), lambda i: (0, i)),
        ],
        out_specs=pl.BlockSpec((outs, part), lambda i: (0, i)),
        out_shape=jax.ShapeDtypeStruct((outs, width), BF16),
        compiler_params=pltpu.CompilerParams(vmem_limit_bytes=32 * 2**20),
        cost_estimate=pl.CostEstimate(
            flops=2 * outs * rows * width,
            bytes_accessed=2 * (outs + width) * rows + 2 * outs * width,
            transcendentals=0,
        ),
    )(weight, x)


def gather_all(x, axis):
    shards = lax.axis_size(axis)
    return lax.all_to_all(jnp.broadcast_to(x[None], (shards,) + x.shape), axis, 0, 0, tiled=True)


def body(tokens, target, task_embed, head_a, head_b, base_v, block_tenant, block_count):
    groups = lax.axis_size("dp")
    group_now = lax.axis_index("dp")
    tenants, hidden = task_embed.shape
    rank_part = head_a.shape[1]
    width = head_a.shape[2]
    kv_part = head_b.shape[2]
    rows = tokens.shape[0]
    blocks = rows // BLOCK

    shards = lax.axis_size("tensor")
    shard_now = lax.axis_index("tensor")
    full_v = lax.all_gather(base_v, "dp", axis=1, tiled=True)
    kv = full_v.shape[1]

    place = owner_tables(block_tenant, tenants, blocks, groups)
    place_bf = place.astype(BF16)
    slot_rows = dot(place_bf.reshape(groups * SLOTS, tenants), task_embed).astype(BF16)
    slot_rows = jnp.broadcast_to(
        slot_rows.reshape(groups, 1, SLOTS, hidden), (groups, rank_part, SLOTS, hidden)
    ).reshape(groups * rank_part * SLOTS, hidden)

    flat_b = generate(slot_rows, head_b, SLOTS)
    own_b_cols = lax.all_to_all(
        flat_b.reshape(groups, rank_part * SLOTS, kv_part), "dp", 0, 0, tiled=True
    ).reshape(R * SLOTS, kv_part)
    wide = spread_embed(slot_rows.T, rank_part)
    slot_rows, own_b_cols, wide = lax.optimization_barrier((slot_rows, own_b_cols, wide))
    every_b = gather_all(own_b_cols, "tensor")
    flat_a = generate(slot_rows, head_a, SLOTS)
    flat_a, every_b = lax.optimization_barrier((flat_a, every_b))
    own_a = lax.all_to_all(
        flat_a.reshape(groups, rank_part * SLOTS, width), "dp", 0, 0, tiled=True
    ).reshape(R * SLOTS, width)

    mine = lax.dynamic_index_in_dim(place_bf, group_now, 0, keepdims=False)
    flat_own_b = jnp.transpose(every_b, (1, 0, 2)).reshape(R * SLOTS, kv)
    own_b = flat_own_b.reshape(R, SLOTS, kv)
    gram_b = jnp.einsum("rsc,qsc->srq", own_b, own_b, preferred_element_type=F32)
    through = dot_nt(flat_own_b, full_v).astype(BF16)

    own_blocks = lax.dynamic_slice_in_dim(block_tenant, group_now * blocks, blocks)
    tenant_hot = own_blocks[:, None] == jnp.arange(tenants, dtype=jnp.int32)[None, :]
    pick = jnp.sum(
        (mine.astype(F32)[:, None, :] * tenant_hot[None, :, :].astype(F32)), axis=2
    )
    count = block_count.astype(F32)
    slot_count = jnp.sum(mine.astype(F32) * count[None, :], axis=1)
    slot_weight = 1.0 / (BLOCK * jnp.maximum(slot_count, 1.0))
    block_weight = 1.0 / (BLOCK * jnp.sum(jnp.where(tenant_hot, count[None, :], 0.0), axis=1))

    pick_rows = jnp.repeat(pick, BLOCK, axis=1)
    partial_t = dot_nt(own_b_cols, target).reshape(R, SLOTS, rows)
    partial_t = jnp.sum(partial_t * pick_rows[None], axis=1)
    partial_z = dot_nt(through, tokens).reshape(R, SLOTS, rows)
    partial_z = jnp.sum(partial_z * pick_rows[None], axis=1) - partial_t
    own_a, partial_z = lax.optimization_barrier((own_a, partial_z))
    partial_l = dot_nt(own_a, tokens).reshape(R, SLOTS, rows)
    partial_l = jnp.sum(partial_l * pick_rows[None], axis=1)
    both = jnp.concatenate([partial_l, partial_z], axis=0).astype(BF16)
    both = jnp.sum(gather_all(both, "tensor").astype(F32), axis=0)
    low_rank = both[:R].astype(BF16)
    back = both[R:].reshape(R, blocks, BLOCK)
    low_blocks = low_rank.reshape(R, blocks, BLOCK)
    gram_block = jnp.einsum(
        "sb,srq->brq", pick, gram_b, precision=lax.Precision.HIGHEST
    )
    cross = jnp.einsum(
        "brq,qbm->rbm", gram_block.astype(BF16), low_blocks, preferred_element_type=F32
    )
    rank_grad = (back + 2.0 * cross) * block_weight[None, :, None]
    rank_grad = rank_grad.astype(BF16).reshape(R, rows)

    pick_bf = pick_rows.astype(BF16)
    spread_g = (2.0 * rank_grad[:, None, :] * pick_bf[None]).reshape(R * SLOTS, rows)
    spread_l = (low_rank[:, None, :] * pick_bf[None]).reshape(R * SLOTS, rows)
    mixed = mix(jnp.concatenate([spread_g, spread_l], axis=0), tokens)
    grad_a, low_x = mixed[: R * SLOTS], mixed[R * SLOTS :]
    every_a = lax.all_to_all(
        grad_a.reshape(groups, rank_part * SLOTS, width), "dp", 0, 0, tiled=True
    ).reshape(groups * rank_part * SLOTS, width)

    gram_l = jnp.einsum("rbm,qbm->brq", low_blocks, low_blocks, preferred_element_type=F32)
    gram_l = jnp.einsum("sb,brq->srq", pick, gram_l, precision=lax.Precision.HIGHEST)
    adapted = jnp.einsum(
        "srq,qsc->rsc",
        gram_l.astype(BF16),
        own_b_cols.reshape(R, SLOTS, kv_part),
        preferred_element_type=F32,
    )
    extra = 2.0 * adapted.reshape(R * SLOTS, kv_part) - dot(spread_l, target)
    here = (jnp.arange(shards) == shard_now).astype(F32)
    scale = jnp.tile(2.0 * slot_weight, (R,))
    grad_b = dot(low_x, full_v).reshape(R * SLOTS, shards, kv_part)
    grad_b = (grad_b + here[None, :, None] * extra[:, None, :]) * scale[:, None, None]
    grad_b = grad_b.astype(BF16).reshape(groups, rank_part * SLOTS, shards, kv_part)
    grad_b = jnp.transpose(grad_b, (0, 2, 1, 3))
    grad_b = grad_b.reshape(groups * shards, rank_part * SLOTS, kv_part)
    every_gb = lax.all_to_all(grad_b, ("dp", "tensor"), 0, 0, tiled=True)
    every_gb = every_gb.reshape(groups, shards, rank_part * SLOTS, kv_part).astype(F32)
    every_gb = jnp.sum(every_gb, axis=1).astype(BF16)
    every_gb = every_gb.reshape(groups * rank_part * SLOTS, kv_part)

    grad_head_a = head_grad(wide, every_a, rank_part)
    grad_head_b = head_grad(wide, every_gb, rank_part)
    return (grad_head_a, grad_head_b)


def solution(mesh):
    return jax.shard_map(
        body,
        mesh=mesh,
        in_specs=(
            P(("parts", "dp"), "tensor"),
            P(("parts", "dp"), "tensor"),
            P("parts", None),
            P(None, "dp", "tensor"),
            P(None, "dp", "tensor"),
            P("tensor", "dp"),
            P("parts"),
            P("parts"),
        ),
        out_specs=(P("parts", "dp", "tensor"), P("parts", "dp", "tensor")),
        check_vma=False,
    )
```
